32 devices in a mesh: seq: 8 (over y, x, core), head: 4 (over z).
Axes of the slice: x: 2, y: 2, z: 4, core: 2. Of those that a mesh axis runs over, the one named last changes fastest.
Arguments:
- queries: bfloat16 [16384, 512], P('seq', 'head'), may hold values from -4 to 4
- key_rows: bfloat16 [16384, 512], P('seq', 'head'), may hold values from -4 to 4
- value_rows: bfloat16 [16384, 512], P('seq', 'head'), may hold values from -6 to 6
- norm_gain: float32 [512], P('head'), may hold values from 0.1 to 1.9
- out_grad: bfloat16 [16384, 512], P('seq', 'head'), may hold values from -6 to 6
Outputs:
- normed: bfloat16 [16384, 512], P('seq', 'head')
- query_grad: bfloat16 [16384, 512], P('seq', 'head')
- key_grad: bfloat16 [16384, 512], P('seq', 'head')
- value_grad: bfloat16 [16384, 512], P('seq', 'head')
The draws below stay inside these ranges and needn't reach their ends.
All inputs are finite; a program needn't handle non-finite values.
Results may differ from the reference program's by a relative error of at most 0.0059.
Values sent between devices are 32-bit elements; how exact they have to be, the bound alone decides.
A program may use at most 64 MiB of HBM per device.

```python
import jax
import jax.numpy as jnp
from jax import lax

HEAD_DIM = 128
BLOCK = 512
HEADS = 4
WIDTH = 512
TOKENS = 16384
NB = 32


def levels(rng, shape, pieces, least, largest):
    level, own = 1.0, jax.random.fold_in(rng, 6)
    for position, parts in pieces:
        draws = jnp.exp(jax.random.uniform(jax.random.fold_in(own, position), (parts,), jnp.float32, least / len(pieces), largest / len(pieces)))
        level = level * jnp.repeat(draws, shape[position] // parts).reshape([-1 if axis == position else 1 for axis in range(len(shape))])
    return level


def noise(stream_key, shape, scale, reach, split=(), held_as=jnp.bfloat16):
    values = scale * jax.random.normal(stream_key, shape, jnp.float32)
    if split:
        values = values * levels(stream_key, shape, split, -0.22, 0.18)
    return jnp.clip(values, -reach, reach).astype(held_as)


def setup_inputs(seed: int = 0) -> dict:
    keys = jax.random.split(jax.random.key(seed), 6)
    queries = noise(keys[0], (TOKENS, WIDTH), 0.3, 4.0, ((0, 8), (1, 4)))
    key_rows = noise(keys[1], (TOKENS, WIDTH), 0.3, 4.0, ((0, 8), (1, 4)))
    value_rows = noise(keys[2], (TOKENS, WIDTH), 1.0, 6.0, ((0, 8), (1, 4)))
    norm_gain = jnp.clip(1.0 + 0.18 * jax.random.normal(keys[3], (WIDTH,), jnp.float32), 0.1, 1.9)
    out_grad = noise(keys[4], (TOKENS, WIDTH), 1.0, 6.0, ((0, 8), (1, 4)))
    return dict(queries=queries, key_rows=key_rows, value_rows=value_rows, norm_gain=norm_gain, out_grad=out_grad)


def causal_mask(size):
    row_index = lax.broadcasted_iota(jnp.int32, (size, size), 0)
    col_index = lax.broadcasted_iota(jnp.int32, (size, size), 1)
    return row_index >= col_index

def split_heads(array):
    return array.reshape(NB, BLOCK, HEADS, HEAD_DIM).transpose(2, 0, 1, 3)

def join_heads(array):
    return array.transpose(1, 2, 0, 3).reshape(TOKENS, HEADS * HEAD_DIM)

def forward_head(operands):
    query, key_in, value = operands
    query_f = query.astype(jnp.float32)
    key_f = key_in.astype(jnp.float32)
    value_f = value.astype(jnp.float32)
    states = jnp.einsum('bsd,bse->bde', key_f, value_f)
    running = jnp.cumsum(states, 0)
    prefix = jnp.concatenate([jnp.zeros_like(states[:1]), running[:-1]], 0).astype(jnp.bfloat16)
    scores = jnp.einsum('btd,bsd->bts', query_f, key_f)
    attn = jnp.where(causal_mask(BLOCK)[None], scores, 0.0).astype(jnp.bfloat16)
    output = jnp.einsum('bts,bse->bte', attn.astype(jnp.float32), value_f)
    output = output + jnp.einsum('btd,bde->bte', query_f, prefix.astype(jnp.float32))
    return (output, prefix)

def backward_head(operands):
    query, key_in, value, dout, prefix = operands
    query_f = query.astype(jnp.float32)
    key_f = key_in.astype(jnp.float32)
    value_f = value.astype(jnp.float32)
    dout_f = dout.astype(jnp.float32)
    mask = causal_mask(BLOCK)[None]
    grad_states = jnp.einsum('btd,bte->bde', query_f, dout_f)
    behind = jnp.cumsum(grad_states[::-1], 0)[::-1]
    suffix = jnp.concatenate([behind[1:], jnp.zeros_like(grad_states[:1])], 0).astype(jnp.bfloat16)
    suffix_f = suffix.astype(jnp.float32)
    prefix_f = prefix.astype(jnp.float32)
    scores = jnp.einsum('btd,bsd->bts', query_f, key_f)
    attn = jnp.where(mask, scores, 0.0).astype(jnp.bfloat16).astype(jnp.float32)
    bmat = jnp.where(mask, jnp.einsum('bte,bse->bts', dout_f, value_f), 0.0).astype(jnp.bfloat16).astype(jnp.float32)
    query_grad = jnp.einsum('bts,bsd->btd', bmat, key_f) + jnp.einsum('bte,bde->btd', dout_f, prefix_f)
    key_grad = jnp.einsum('bts,btd->bsd', bmat, query_f) + jnp.einsum('bse,bde->bsd', value_f, suffix_f)
    value_grad = jnp.einsum('bts,bte->bse', attn, dout_f) + jnp.einsum('bsd,bde->bse', key_f, suffix_f)
    return (query_grad.astype(jnp.bfloat16), key_grad.astype(jnp.bfloat16), value_grad.astype(jnp.bfloat16))

def reference(queries, key_rows, value_rows, norm_gain, out_grad):
    query4 = split_heads(queries)
    key4 = split_heads(key_rows)
    value4 = split_heads(value_rows)
    output, prefix = lax.map(forward_head, (query4, key4, value4))
    width_all = HEADS * HEAD_DIM
    squares = lax.optimization_barrier(jnp.sum(output * output, axis=(0, 3)))
    rstd = lax.rsqrt(squares / width_all + 1e-05)[None, :, :, None]
    gain4 = norm_gain.astype(jnp.float32).reshape(HEADS, 1, 1, HEAD_DIM)
    normed = (output * rstd * gain4).astype(jnp.bfloat16)
    scaled = split_heads(out_grad).astype(jnp.float32) * gain4
    mean_prod = (lax.optimization_barrier(jnp.sum(scaled * output, axis=(0, 3))) / width_all)[None, :, :, None]
    dout = (rstd * scaled - output * rstd ** 3 * mean_prod).astype(jnp.bfloat16)
    query_grad, key_grad, value_grad = lax.map(backward_head, (query4, key4, value4, dout, prefix))
    return (join_heads(normed), join_heads(query_grad), join_heads(key_grad), join_heads(value_grad))
```

```python
import functools

import jax
import jax.numpy as jnp
from jax import lax
from jax.experimental import pallas as pl
from jax.experimental.pallas import tpu as pltpu
from jax.sharding import PartitionSpec as P

HEAD_DIM = 128
CHUNK = 256
EPS = 1e-05
MESH = pl.DeviceIdType.MESH
F32 = jnp.float32
BF16 = jnp.bfloat16


def dot(a, b, dim_a, dim_b):
    return lax.dot_general(a, b, (((dim_a,), (dim_b,)), ((), ())), preferred_element_type=F32)


def iota2(rows, columns):
    return (
        lax.broadcasted_iota(jnp.int32, (rows, columns), 0),
        lax.broadcasted_iota(jnp.int32, (rows, columns), 1),
    )


def exchange(total, pair_in, half_out, slots, half_acc, half_in, sems, chip, core, chips, upward):
    pair_s, pair_r, chip_s, chip_r, half_s, half_r = sems
    half = HEAD_DIM // 2
    mine = pl.ds(pl.multiple_of(core * half, half), half)
    partner = {"seq": chip * 2 + (1 - core)}

    def pair_copy():
        return pltpu.make_async_remote_copy(
            total, pair_in, pair_s, pair_r, device_id=partner, device_id_type=MESH
        )

    def chip_copy(slot, to):
        return pltpu.make_async_remote_copy(
            half_out, slots.at[slot], chip_s.at[to], chip_r.at[slot],
            device_id={"seq": to * 2 + core}, device_id_type=MESH,
        )

    def half_copy():
        return pltpu.make_async_remote_copy(
            half_acc, half_in, half_s, half_r, device_id=partner, device_id_type=MESH
        )

    def ahead(other):
        return (other > chip) if upward else (other < chip)

    def start_pair():
        pair_copy().start()

    def start_chips():
        pair_copy().wait_recv()
        half_out[...] = total[mine, :] + pair_in[mine, :]
        for step in range(1, chips):
            to = lax.rem(chip + step, chips)

            @pl.when(ahead(to))
            def _():
                chip_copy(chip, to).start()

    def start_halves():
        half_acc[...] = jnp.zeros_like(half_acc)
        for source in range(chips):

            @pl.when(jnp.logical_and(jnp.logical_not(ahead(source)), source != chip))
            def _():
                chip_copy(source, source).wait_recv()
                half_acc[...] += slots[source]

        half_copy().start()

    def finish(result):
        half_copy().wait_recv()
        result[mine, :] = half_acc[...]
        result[pl.ds(pl.multiple_of((1 - core) * half, half), half), :] = half_in[...]

        @pl.when(core == (1 if upward else 0))
        def _():
            result[...] += pair_in[...]

    def drain():
        pair_copy().wait_send()
        for to in range(chips):

            @pl.when(ahead(to))
            def _():
                chip_copy(chip, to).wait_send()

        half_copy().wait_send()

    return start_pair, start_chips, start_halves, finish, drain


def kernel(
    chips, heads, width_all,
    q_hbm, k_hbm, v_hbm, gain_ref, g_hbm,
    normed_hbm, qg_hbm, kg_hbm, vg_hbm,
    q, k, v, g, normed, qg, kg, vg,
    out32, attn_t, q_t, dout, prefix16, before, after, kpart, vpart,
    stats, stat_slots, scale_rows,
    total_f, pair_f, hout_f, slots_f, hacc_f, hin_f, earlier,
    total_b, pair_b, hout_b, slots_b, hacc_b, hin_b, later,
    in_sem, out_sem, stat_s, stat_r,
    pair_s, pair_r, chip_s, chip_r, half_s, half_r,
):
    seq_index = lax.axis_index("seq")
    head_index = lax.axis_index("head")
    chip = lax.div(seq_index, 2)
    core = lax.rem(seq_index, 2)
    tokens = q.shape[0]
    chunks = tokens // CHUNK
    groups = CHUNK // HEAD_DIM
    stat_rows = tokens // HEAD_DIM

    loads = [
        pltpu.make_async_copy(src, dst, in_sem.at[i])
        for i, (src, dst) in enumerate(((k_hbm, k), (v_hbm, v), (q_hbm, q), (g_hbm, g)))
    ]
    for load in loads:
        load.start()

    barrier = pltpu.get_barrier_semaphore()
    pl.semaphore_signal(
        barrier, inc=1, device_id={"seq": chip * 2 + (1 - core)}, device_id_type=MESH
    )
    for step in range(1, chips):
        pl.semaphore_signal(
            barrier, inc=1,
            device_id={"seq": lax.rem(chip + step, chips) * 2 + core}, device_id_type=MESH,
        )
    for step in range(1, heads):
        pl.semaphore_signal(
            barrier, inc=1, device_id={"head": lax.rem(head_index + step, heads)},
            device_id_type=MESH,
        )

    def rows(c):
        return pl.ds(pl.multiple_of(c * CHUNK, CHUNK), CHUNK)

    def sems(i):
        return (
            pair_s.at[i], pair_r.at[i], chip_s.at[i], chip_r.at[i], half_s.at[i], half_r.at[i]
        )

    forward = exchange(
        total_f, pair_f, hout_f, slots_f, hacc_f, hin_f, sems(0), chip, core, chips, True
    )
    backward = exchange(
        total_b, pair_b, hout_b, slots_b, hacc_b, hin_b, sems(1), chip, core, chips, False
    )

    loads[0].wait()
    loads[1].wait()
    running = jnp.zeros((HEAD_DIM, HEAD_DIM), F32)
    for c in range(chunks):
        before[c] = running
        running = running + dot(k[rows(c), :], v[rows(c), :], 0, 0)
    total_f[...] = running

    pl.semaphore_wait(barrier, 1 + (chips - 1) + (heads - 1))
    forward[0]()

    row, column = iota2(CHUNK, CHUNK)

    def local_output(c, carry):
        scores = dot(q[rows(c), :], k[rows(c), :], 1, 1)
        attn = jnp.where(row >= column, scores, 0.0).astype(BF16)
        out32[rows(c), :] = dot(attn, v[rows(c), :], 1, 0)
        return carry

    first = chunks // 4
    loads[2].wait()
    lax.fori_loop(0, first, local_output, 0, unroll=True)
    forward[1]()
    lax.fori_loop(first, chunks, local_output, 0, unroll=2)
    loads[3].wait()
    forward[2]()
    forward[3](earlier)

    eye_row, eye_column = iota2(HEAD_DIM, HEAD_DIM)
    eye = eye_row == eye_column
    gain = gain_ref[...]

    def finish_output(c, carry):
        prefix = (earlier[...] + before[c]).astype(BF16)
        prefix16[c] = prefix
        output = out32[rows(c), :] + dot(q[rows(c), :], prefix, 1, 0)
        out32[rows(c), :] = output
        scaled = g[rows(c), :].astype(F32) * gain
        square = jnp.sum(output * output, axis=1, keepdims=True)
        product = jnp.sum(scaled * output, axis=1, keepdims=True)
        for i in range(groups):
            part = slice(i * HEAD_DIM, (i + 1) * HEAD_DIM)
            stats[pl.ds(c * groups + i, 1), :] = jnp.sum(
                jnp.where(eye, square[part], 0.0), axis=0, keepdims=True
            )
            stats[pl.ds(stat_rows + c * groups + i, 1), :] = jnp.sum(
                jnp.where(eye, product[part], 0.0), axis=0, keepdims=True
            )
        return carry

    lax.fori_loop(0, chunks, finish_output, 0, unroll=2)

    def stat_copy(slot, to):
        return pltpu.make_async_remote_copy(
            stats, stat_slots.at[slot], stat_s.at[to], stat_r.at[slot],
            device_id={"head": to}, device_id_type=MESH,
        )

    for step in range(1, heads):
        to = lax.rem(head_index + step, heads)
        stat_copy(head_index, to).start()

    def transposed(c, carry):
        scores = dot(k[rows(c), :], q[rows(c), :], 1, 1)
        attn_t[c] = jnp.where(row <= column, scores, 0.0).astype(BF16)
        q_t[c] = q[rows(c), :].T
        return carry

    lax.fori_loop(0, chunks, transposed, 0, unroll=2)

    total = stats[...]
    for step in range(1, heads):
        source = lax.rem(head_index + step, heads)
        stat_copy(source, source).wait_recv()
        total = total + stat_slots[source]
    total = total * (1.0 / width_all)
    rstd = lax.rsqrt(total[:stat_rows] + EPS)
    scale_rows[:stat_rows] = rstd
    scale_rows[stat_rows:] = rstd * rstd * rstd * total[stat_rows:]

    def spread(r):
        return jnp.sum(jnp.where(eye, scale_rows[pl.ds(r, 1), :], 0.0), axis=1, keepdims=True)

    def columns(c, offset):
        return jnp.concatenate([spread(offset + c * groups + i) for i in range(groups)], axis=0)

    def gradient(i, running):
        c = chunks - 1 - i
        rstd_c = columns(c, 0)
        output = out32[rows(c), :]
        scaled = g[rows(c), :].astype(F32) * gain
        grad = (rstd_c * scaled - output * columns(c, stat_rows)).astype(BF16)
        dout[rows(c), :] = grad
        normed[rows(c), :] = (output * rstd_c * gain).astype(BF16)
        after[c] = running
        return running + dot(q_t[c], grad, 1, 0)

    total_b[...] = lax.fori_loop(
        0, chunks, gradient, jnp.zeros((HEAD_DIM, HEAD_DIM), F32), unroll=2
    )
    backward[0]()
    stores = [
        pltpu.make_async_copy(src, dst, out_sem.at[i])
        for i, (src, dst) in enumerate(
            ((normed, normed_hbm), (qg, qg_hbm), (kg, kg_hbm), (vg, vg_hbm))
        )
    ]
    stores[0].start()

    def local_gradients(c, carry):
        grad = dout[rows(c), :]
        value = v[rows(c), :]
        bmat = jnp.where(row >= column, dot(grad, value, 1, 1), 0.0).astype(BF16)
        bmat_t = jnp.where(row <= column, dot(value, grad, 1, 1), 0.0).astype(BF16)
        qg[rows(c), :] = (
            dot(bmat, k[rows(c), :], 1, 0) + dot(grad, prefix16[c], 1, 1)
        ).astype(BF16)
        kpart[rows(c), :] = dot(bmat_t, q[rows(c), :], 1, 0)
        vpart[rows(c), :] = dot(attn_t[c], grad, 1, 0)
        return carry

    lax.fori_loop(0, first, local_gradients, 0, unroll=True)
    backward[1]()
    lax.fori_loop(first, chunks, local_gradients, 0, unroll=2)
    stores[1].start()
    backward[2]()
    backward[3](later)

    def finish_gradients(c, carry):
        suffix = (later[...] + after[c]).astype(BF16)
        kg[rows(c), :] = (kpart[rows(c), :] + dot(v[rows(c), :], suffix, 1, 1)).astype(BF16)
        vg[rows(c), :] = (vpart[rows(c), :] + dot(k[rows(c), :], suffix, 1, 0)).astype(BF16)
        return carry

    lax.fori_loop(0, chunks, finish_gradients, 0, unroll=2)
    stores[2].start()
    stores[3].start()
    forward[4]()
    backward[4]()
    for step in range(1, heads):
        to = lax.rem(head_index + step, heads)
        stat_copy(head_index, to).wait_send()
    for store in stores:
        store.wait()


def body(queries, key_rows, value_rows, norm_gain, out_grad):
    tokens, width = queries.shape
    assert width == HEAD_DIM and tokens % CHUNK == 0
    chips = lax.axis_size("seq") // 2
    heads = lax.axis_size("head")
    chunks = tokens // CHUNK
    stat_rows = 2 * tokens // HEAD_DIM
    wide = (tokens, width)
    square = (HEAD_DIM, HEAD_DIM)
    half = (HEAD_DIM // 2, HEAD_DIM)
    link = [
        pltpu.VMEM(square, F32),
        pltpu.VMEM(square, F32),
        pltpu.VMEM(half, F32),
        pltpu.VMEM((chips,) + half, F32),
        pltpu.VMEM(half, F32),
        pltpu.VMEM(half, F32),
        pltpu.VMEM(square, F32),
    ]
    hbm = pl.BlockSpec(memory_space=pl.ANY)
    dma = pltpu.SemaphoreType.DMA
    return pl.pallas_call(
        functools.partial(kernel, chips, heads, width * heads),
        out_shape=[jax.ShapeDtypeStruct(wide, BF16)] * 4,
        in_specs=[hbm, hbm, hbm, pl.BlockSpec(memory_space=pltpu.VMEM), hbm],
        out_specs=[hbm] * 4,
        scratch_shapes=[pltpu.VMEM(wide, BF16)] * 8
        + [
            pltpu.VMEM(wide, F32),
            pltpu.VMEM((chunks, CHUNK, CHUNK), BF16),
            pltpu.VMEM((chunks, HEAD_DIM, CHUNK), BF16),
            pltpu.VMEM(wide, BF16),
            pltpu.VMEM((chunks,) + square, BF16),
            pltpu.VMEM((chunks,) + square, F32),
            pltpu.VMEM((chunks,) + square, F32),
            pltpu.VMEM(wide, F32),
            pltpu.VMEM(wide, F32),
            pltpu.VMEM((stat_rows, HEAD_DIM), F32),
            pltpu.VMEM((heads, stat_rows, HEAD_DIM), F32),
            pltpu.VMEM((stat_rows, HEAD_DIM), F32),
        ]
        + link
        + link
        + [
            dma((4,)), dma((4,)), dma((heads,)), dma((heads,)),
            dma((2,)), dma((2,)), dma((2, chips)), dma((2, chips)), dma((2,)), dma((2,)),
        ],
        compiler_params=pltpu.CompilerParams(
            collective_id=0, has_side_effects=True, vmem_limit_bytes=48 * 1024 * 1024
        ),
    )(queries, key_rows, value_rows, norm_gain.reshape(1, width), out_grad)


def solution(mesh):
    spec = P("seq", "head")
    return jax.shard_map(
        body,
        mesh=mesh,
        in_specs=(spec, spec, spec, P("head"), spec),
        out_specs=(spec,) * 4,
        check_vma=False,
    )
```

```python
import functools

import jax
import jax.numpy as jnp
from jax import lax
from jax.experimental import pallas as pl
from jax.experimental.pallas import tpu as pltpu
from jax.sharding import PartitionSpec as P

HEAD_DIM = 128
CHUNK = 256
EPS = 1e-05
MESH = pl.DeviceIdType.MESH
F32 = jnp.float32
BF16 = jnp.bfloat16


def dot(a, b, dim_a, dim_b):
    return lax.dot_general(a, b, (((dim_a,), (dim_b,)), ((), ())), preferred_element_type=F32)


def iota2(rows, columns):
    return (
        lax.broadcasted_iota(jnp.int32, (rows, columns), 0),
        lax.broadcasted_iota(jnp.int32, (rows, columns), 1),
    )


def exchange(total, pair_in, half_out, slots, half_acc, half_in, sems, chip, core, chips, upward):
    pair_s, pair_r, chip_s, chip_r, half_s, half_r = sems
    half = HEAD_DIM // 2
    mine = pl.ds(pl.multiple_of(core * half, half), half)
    partner = {"seq": chip * 2 + (1 - core)}

    def pair_copy():
        return pltpu.make_async_remote_copy(
            total, pair_in, pair_s, pair_r, device_id=partner, device_id_type=MESH
        )

    def chip_copy(slot, to):
        return pltpu.make_async_remote_copy(
            half_out, slots.at[slot], chip_s.at[to], chip_r.at[slot],
            device_id={"seq": to * 2 + core}, device_id_type=MESH,
        )

    def half_copy():
        return pltpu.make_async_remote_copy(
            half_acc, half_in, half_s, half_r, device_id=partner, device_id_type=MESH
        )

    def ahead(other):
        return (other > chip) if upward else (other < chip)

    def start_pair():
        pair_copy().start()

    def start_chips():
        pair_copy().wait_recv()
        half_out[...] = total[mine, :] + pair_in[mine, :]
        for step in range(1, chips):
            to = lax.rem(chip + step, chips)

            @pl.when(ahead(to))
            def _():
                chip_copy(chip, to).start()

    def start_halves():
        half_acc[...] = jnp.zeros_like(half_acc)
        for source in range(chips):

            @pl.when(jnp.logical_and(jnp.logical_not(ahead(source)), source != chip))
            def _():
                chip_copy(source, source).wait_recv()
                half_acc[...] += slots[source]

        half_copy().start()

    def finish(result):
        half_copy().wait_recv()
        result[mine, :] = half_acc[...]
        result[pl.ds(pl.multiple_of((1 - core) * half, half), half), :] = half_in[...]

        @pl.when(core == (1 if upward else 0))
        def _():
            result[...] += pair_in[...]

    def drain():
        pair_copy().wait_send()
        for to in range(chips):

            @pl.when(ahead(to))
            def _():
                chip_copy(chip, to).wait_send()

        half_copy().wait_send()

    return start_pair, start_chips, start_halves, finish, drain


def kernel(
    chips, heads, width_all,
    q_hbm, k_hbm, v_hbm, gain_hbm, g_hbm,
    normed, qg, kpart, vpart, suffix16, k, v,
    q, g, gain_ref,
    out32, attn_t, q_t, dout, prefix16, before, after,
    stats, stat_slots, scale_rows,
    total_f, pair_f, hout_f, slots_f, hacc_f, hin_f, earlier,
    total_b, pair_b, hout_b, slots_b, hacc_b, hin_b, later,
    in_sem, stat_s, stat_r,
    pair_s, pair_r, chip_s, chip_r, half_s, half_r,
):
    seq_index = lax.axis_index("seq")
    head_index = lax.axis_index("head")
    chip = lax.div(seq_index, 2)
    core = lax.rem(seq_index, 2)
    tokens = q.shape[0]
    chunks = tokens // CHUNK
    groups = CHUNK // HEAD_DIM
    stat_rows = tokens // HEAD_DIM

    loads = [
        pltpu.make_async_copy(src, dst, in_sem.at[i])
        for i, (src, dst) in enumerate(
            ((k_hbm, k), (v_hbm, v), (q_hbm, q), (g_hbm, g), (gain_hbm, gain_ref))
        )
    ]
    for load in loads:
        load.start()

    barrier = pltpu.get_barrier_semaphore()
    pl.semaphore_signal(
        barrier, inc=1, device_id={"seq": chip * 2 + (1 - core)}, device_id_type=MESH
    )
    for step in range(1, chips):
        pl.semaphore_signal(
            barrier, inc=1,
            device_id={"seq": lax.rem(chip + step, chips) * 2 + core}, device_id_type=MESH,
        )
    for step in range(1, heads):
        pl.semaphore_signal(
            barrier, inc=1, device_id={"head": lax.rem(head_index + step, heads)},
            device_id_type=MESH,
        )

    def rows(c):
        return pl.ds(pl.multiple_of(c * CHUNK, CHUNK), CHUNK)

    def sems(i):
        return (
            pair_s.at[i], pair_r.at[i], chip_s.at[i], chip_r.at[i], half_s.at[i], half_r.at[i]
        )

    forward = exchange(
        total_f, pair_f, hout_f, slots_f, hacc_f, hin_f, sems(0), chip, core, chips, True
    )
    backward = exchange(
        total_b, pair_b, hout_b, slots_b, hacc_b, hin_b, sems(1), chip, core, chips, False
    )

    loads[0].wait()
    loads[1].wait()
    running = jnp.zeros((HEAD_DIM, HEAD_DIM), F32)
    for c in range(chunks):
        before[c] = running
        running = running + dot(k[rows(c), :], v[rows(c), :], 0, 0)
    total_f[...] = running

    pl.semaphore_wait(barrier, 1 + (chips - 1) + (heads - 1))
    forward[0]()

    row, column = iota2(CHUNK, CHUNK)

    def local_output(c, carry):
        scores = dot(q[rows(c), :], k[rows(c), :], 1, 1)
        attn = jnp.where(row >= column, scores, 0.0).astype(BF16)
        out32[rows(c), :] = dot(attn, v[rows(c), :], 1, 0)
        return carry

    first = chunks // 4
    loads[2].wait()
    lax.fori_loop(0, first, local_output, 0, unroll=True)
    forward[1]()
    lax.fori_loop(first, chunks, local_output, 0, unroll=2)
    loads[3].wait()
    loads[4].wait()
    forward[2]()
    forward[3](earlier)

    eye_row, eye_column = iota2(HEAD_DIM, HEAD_DIM)
    eye = eye_row == eye_column
    gain = gain_ref[...]

    def finish_output(c, carry):
        prefix = (earlier[...] + before[c]).astype(BF16)
        prefix16[c] = prefix
        output = out32[rows(c), :] + dot(q[rows(c), :], prefix, 1, 0)
        out32[rows(c), :] = output
        scaled = g[rows(c), :].astype(F32) * gain
        square = jnp.sum(output * output, axis=1, keepdims=True)
        product = jnp.sum(scaled * output, axis=1, keepdims=True)
        for i in range(groups):
            part = slice(i * HEAD_DIM, (i + 1) * HEAD_DIM)
            stats[pl.ds(c * groups + i, 1), :] = jnp.sum(
                jnp.where(eye, square[part], 0.0), axis=0, keepdims=True
            )
            stats[pl.ds(stat_rows + c * groups + i, 1), :] = jnp.sum(
                jnp.where(eye, product[part], 0.0), axis=0, keepdims=True
            )
        return carry

    lax.fori_loop(0, chunks, finish_output, 0, unroll=2)

    def stat_copy(slot, to):
        return pltpu.make_async_remote_copy(
            stats, stat_slots.at[slot], stat_s.at[to], stat_r.at[slot],
            device_id={"head": to}, device_id_type=MESH,
        )

    for step in range(1, heads):
        to = lax.rem(head_index + step, heads)
        stat_copy(head_index, to).start()

    def transposed(c, carry):
        scores = dot(k[rows(c), :], q[rows(c), :], 1, 1)
        attn_t[c] = jnp.where(row <= column, scores, 0.0).astype(BF16)
        q_t[c] = q[rows(c), :].T
        return carry

    lax.fori_loop(0, chunks, transposed, 0, unroll=2)

    total = stats[...]
    for step in range(1, heads):
        source = lax.rem(head_index + step, heads)
        stat_copy(source, source).wait_recv()
        total = total + stat_slots[source]
    total = total * (1.0 / width_all)
    rstd = lax.rsqrt(total[:stat_rows] + EPS)
    scale_rows[:stat_rows] = rstd
    scale_rows[stat_rows:] = rstd * rstd * rstd * total[stat_rows:]

    def spread(r):
        return jnp.sum(jnp.where(eye, scale_rows[pl.ds(r, 1), :], 0.0), axis=1, keepdims=True)

    def columns(c, offset):
        return jnp.concatenate([spread(offset + c * groups + i) for i in range(groups)], axis=0)

    def gradient(i, running):
        c = chunks - 1 - i
        rstd_c = columns(c, 0)
        output = out32[rows(c), :]
        scaled = g[rows(c), :].astype(F32) * gain
        grad = (rstd_c * scaled - output * columns(c, stat_rows)).astype(BF16)
        dout[rows(c), :] = grad
        normed[rows(c), :] = (output * rstd_c * gain).astype(BF16)
        after[c] = running
        return running + dot(q_t[c], grad, 1, 0)

    total_b[...] = lax.fori_loop(
        0, chunks, gradient, jnp.zeros((HEAD_DIM, HEAD_DIM), F32), unroll=2
    )
    backward[0]()
    def local_gradients(c, carry):
        grad = dout[rows(c), :]
        value = v[rows(c), :]
        bmat = jnp.where(row >= column, dot(grad, value, 1, 1), 0.0).astype(BF16)
        bmat_t = jnp.where(row <= column, dot(value, grad, 1, 1), 0.0).astype(BF16)
        qg[rows(c), :] = (
            dot(bmat, k[rows(c), :], 1, 0) + dot(grad, prefix16[c], 1, 1)
        ).astype(BF16)
        kpart[rows(c), :] = dot(bmat_t, q[rows(c), :], 1, 0)
        vpart[rows(c), :] = dot(attn_t[c], grad, 1, 0)
        return carry

    lax.fori_loop(0, first, local_gradients, 0, unroll=True)
    backward[1]()
    lax.fori_loop(first, chunks, local_gradients, 0, unroll=2)
    backward[2]()
    backward[3](later)
    for c in range(chunks):
        suffix16[c] = (later[...] + after[c]).astype(BF16)
    forward[4]()
    backward[4]()
    for step in range(1, heads):
        to = lax.rem(head_index + step, heads)
        stat_copy(head_index, to).wait_send()


def last_kernel(
    normed, qg, kpart, vpart, suffix16, k, v, normed_hbm, qg_hbm, kg_hbm, vg_hbm, kg, vg, sem
):
    chunks = k.shape[0] // CHUNK
    parts = 2 if chunks % 2 == 0 else 1
    per_part = chunks // parts
    stores = [
        pltpu.make_async_copy(normed, normed_hbm, sem.at[0]),
        pltpu.make_async_copy(qg, qg_hbm, sem.at[1]),
    ]
    for store in stores:
        store.start()

    def finish_gradients(c, carry):
        part = pl.ds(pl.multiple_of(c * CHUNK, CHUNK), CHUNK)
        suffix = suffix16[c]
        kg[part, :] = (kpart[part, :] + dot(v[part, :], suffix, 1, 1)).astype(BF16)
        vg[part, :] = (vpart[part, :] + dot(k[part, :], suffix, 1, 0)).astype(BF16)
        return carry

    for i in range(parts):
        lax.fori_loop(i * per_part, (i + 1) * per_part, finish_gradients, 0, unroll=2)
        part = pl.ds(i * per_part * CHUNK, per_part * CHUNK)
        for n, (src, dst) in enumerate(((kg, kg_hbm), (vg, vg_hbm))):
            store = pltpu.make_async_copy(src.at[part], dst.at[part], sem.at[2 + 2 * i + n])
            store.start()
            stores.append(store)
    for store in stores:
        store.wait()


def body(queries, key_rows, value_rows, norm_gain, out_grad):
    tokens, width = queries.shape
    assert width == HEAD_DIM and tokens % CHUNK == 0
    chips = lax.axis_size("seq") // 2
    heads = lax.axis_size("head")
    chunks = tokens // CHUNK
    stat_rows = 2 * tokens // HEAD_DIM
    wide = (tokens, width)
    square = (HEAD_DIM, HEAD_DIM)
    half = (HEAD_DIM // 2, HEAD_DIM)
    link = [
        pltpu.VMEM(square, F32),
        pltpu.VMEM(square, F32),
        pltpu.VMEM(half, F32),
        pltpu.VMEM((chips,) + half, F32),
        pltpu.VMEM(half, F32),
        pltpu.VMEM(half, F32),
        pltpu.VMEM(square, F32),
    ]
    hbm = pl.BlockSpec(memory_space=pltpu.HBM)
    vmem = pl.BlockSpec(memory_space=pltpu.VMEM)
    dma = pltpu.SemaphoreType.DMA
    held = pl.pallas_call(
        functools.partial(kernel, chips, heads, width * heads),
        out_shape=[
            jax.ShapeDtypeStruct(wide, BF16),
            jax.ShapeDtypeStruct(wide, BF16),
            jax.ShapeDtypeStruct(wide, F32),
            jax.ShapeDtypeStruct(wide, F32),
            jax.ShapeDtypeStruct((chunks,) + square, BF16),
            jax.ShapeDtypeStruct(wide, BF16),
            jax.ShapeDtypeStruct(wide, BF16),
        ],
        in_specs=[hbm] * 5,
        out_specs=[vmem] * 7,
        scratch_shapes=[
            pltpu.VMEM(wide, BF16),
            pltpu.VMEM(wide, BF16),
            pltpu.VMEM((1, width), F32),
            pltpu.VMEM(wide, F32),
            pltpu.VMEM((chunks, CHUNK, CHUNK), BF16),
            pltpu.VMEM((chunks, HEAD_DIM, CHUNK), BF16),
            pltpu.VMEM(wide, BF16),
            pltpu.VMEM((chunks,) + square, BF16),
            pltpu.VMEM((chunks,) + square, F32),
            pltpu.VMEM((chunks,) + square, F32),
            pltpu.VMEM((stat_rows, HEAD_DIM), F32),
            pltpu.VMEM((heads, stat_rows, HEAD_DIM), F32),
            pltpu.VMEM((stat_rows, HEAD_DIM), F32),
        ]
        + link
        + link
        + [
            dma((5,)), dma((heads,)), dma((heads,)),
            dma((2,)), dma((2,)), dma((2, chips)), dma((2, chips)), dma((2,)), dma((2,)),
        ],
        compiler_params=pltpu.CompilerParams(
            collective_id=0, has_side_effects=True, vmem_limit_bytes=32 * 1024 * 1024
        ),
    )(*[
        pltpu.with_memory_space_constraint(array, pltpu.HBM)
        for array in (queries, key_rows, value_rows, norm_gain.reshape(1, width), out_grad)
    ])
    return pl.pallas_call(
        last_kernel,
        out_shape=[jax.ShapeDtypeStruct(wide, BF16)] * 4,
        in_specs=[vmem] * 7,
        out_specs=[hbm] * 4,
        scratch_shapes=[pltpu.VMEM(wide, BF16), pltpu.VMEM(wide, BF16), dma((6,))],
        compiler_params=pltpu.CompilerParams(vmem_limit_bytes=32 * 1024 * 1024),
    )(*held)


def solution(mesh):
    spec = P("seq", "head")
    return jax.shard_map(
        body,
        mesh=mesh,
        in_specs=(spec, spec, spec, P("head"), spec),
        out_specs=(spec,) * 4,
        check_vma=False,
    )
```

```python
import functools

import jax
import jax.numpy as jnp
from jax import lax
from jax.experimental import pallas as pl
from jax.experimental.pallas import tpu as pltpu
from jax.sharding import PartitionSpec as P

HEAD_DIM = 128
CHUNK = 256
PIECES = 2
UNROLL = 4
EPS = 1e-05
MESH = pl.DeviceIdType.MESH
F32 = jnp.float32
BF16 = jnp.bfloat16


def dot(a, b, dim_a, dim_b):
    return lax.dot_general(a, b, (((dim_a,), (dim_b,)), ((), ())), preferred_element_type=F32)


def iota2(rows, columns):
    return (
        lax.broadcasted_iota(jnp.int32, (rows, columns), 0),
        lax.broadcasted_iota(jnp.int32, (rows, columns), 1),
    )


def exchange(total, pair_in, half_out, slots, half_acc, half_in, sems, chip, core, chips, upward):
    pair_s, pair_r, chip_s, chip_r, half_s, half_r = sems
    half = HEAD_DIM // 2
    mine = pl.ds(pl.multiple_of(core * half, half), half)
    partner = {"seq": chip * 2 + (1 - core)}

    def pair_copy():
        return pltpu.make_async_remote_copy(
            total, pair_in, pair_s, pair_r, device_id=partner, device_id_type=MESH
        )

    def chip_copy(slot, to):
        return pltpu.make_async_remote_copy(
            half_out, slots.at[slot], chip_s.at[to], chip_r.at[slot],
            device_id={"seq": to * 2 + core}, device_id_type=MESH,
        )

    def half_copy():
        return pltpu.make_async_remote_copy(
            half_acc, half_in, half_s, half_r, device_id=partner, device_id_type=MESH
        )

    def ahead(other):
        return (other > chip) if upward else (other < chip)

    def start_pair():
        pair_copy().start()

    def start_chips():
        pair_copy().wait_recv()
        half_out[...] = total[mine, :] + pair_in[mine, :]
        for step in range(1, chips):
            to = lax.rem(chip + step, chips)

            @pl.when(ahead(to))
            def _():
                chip_copy(chip, to).start()

    def start_halves():
        half_acc[...] = jnp.zeros_like(half_acc)
        for source in range(chips):

            @pl.when(jnp.logical_and(jnp.logical_not(ahead(source)), source != chip))
            def _():
                chip_copy(source, source).wait_recv()
                half_acc[...] += slots[source]

        half_copy().start()

    def finish(result):
        half_copy().wait_recv()
        result[mine, :] = half_acc[...]
        result[pl.ds(pl.multiple_of((1 - core) * half, half), half), :] = half_in[...]

        @pl.when(core == (1 if upward else 0))
        def _():
            result[...] += pair_in[...]

    def drain():
        pair_copy().wait_send()
        for to in range(chips):

            @pl.when(ahead(to))
            def _():
                chip_copy(chip, to).wait_send()

        half_copy().wait_send()

    return start_pair, start_chips, start_halves, finish, drain


def kernel(
    chips, heads, width_all,
    q_hbm, k_hbm, v_hbm, gain_hbm, g_hbm,
    normed, qg, kpart, vpart, later16, k, v,
    q, g, gain_ref,
    out32, attn_t, q_t, dout, before, after,
    stats, stat_slots, scale_rows,
    total_f, pair_f, hout_f, slots_f, hacc_f, hin_f, earlier,
    total_b, pair_b, hout_b, slots_b, hacc_b, hin_b, later,
    in_sem, stat_s, stat_r,
    pair_s, pair_r, chip_s, chip_r, half_s, half_r,
):
    seq_index = lax.axis_index("seq")
    head_index = lax.axis_index("head")
    chip = lax.div(seq_index, 2)
    core = lax.rem(seq_index, 2)
    tokens = q.shape[0]
    chunks = tokens // CHUNK
    groups = CHUNK // HEAD_DIM
    per_piece = chunks // PIECES
    stat_rows = per_piece * groups

    loads = [
        pltpu.make_async_copy(src, dst, in_sem.at[i])
        for i, (src, dst) in enumerate(
            ((k_hbm, k), (v_hbm, v), (q_hbm, q), (g_hbm, g), (gain_hbm, gain_ref))
        )
    ]
    for load in loads:
        load.start()

    barrier = pltpu.get_barrier_semaphore()
    pl.semaphore_signal(
        barrier, inc=1, device_id={"seq": chip * 2 + (1 - core)}, device_id_type=MESH
    )
    for step in range(1, chips):
        pl.semaphore_signal(
            barrier, inc=1,
            device_id={"seq": lax.rem(chip + step, chips) * 2 + core}, device_id_type=MESH,
        )
    for step in range(1, heads):
        pl.semaphore_signal(
            barrier, inc=1, device_id={"head": lax.rem(head_index + step, heads)},
            device_id_type=MESH,
        )

    def rows(c):
        return pl.ds(pl.multiple_of(c * CHUNK, CHUNK), CHUNK)

    def sems(i):
        return (
            pair_s.at[i], pair_r.at[i], chip_s.at[i], chip_r.at[i], half_s.at[i], half_r.at[i]
        )

    forward = exchange(
        total_f, pair_f, hout_f, slots_f, hacc_f, hin_f, sems(0), chip, core, chips, True
    )
    backward = exchange(
        total_b, pair_b, hout_b, slots_b, hacc_b, hin_b, sems(1), chip, core, chips, False
    )

    loads[0].wait()
    loads[1].wait()
    running = jnp.zeros((HEAD_DIM, HEAD_DIM), F32)
    for c in range(chunks):
        before[c] = running
        running = running + dot(k[rows(c), :], v[rows(c), :], 0, 0)
    total_f[...] = running

    pl.semaphore_wait(barrier, 1 + (chips - 1) + (heads - 1))
    forward[0]()

    row, column = iota2(CHUNK, CHUNK)

    def local_output(c, carry):
        scores = dot(q[rows(c), :], k[rows(c), :], 1, 1)
        attn = jnp.where(row >= column, scores, 0.0).astype(BF16)
        out32[rows(c), :] = dot(attn, v[rows(c), :], 1, 0) + dot(
            q[rows(c), :], before[c].astype(BF16), 1, 0
        )
        return carry

    first = chunks // 4
    loads[2].wait()
    lax.fori_loop(0, first, local_output, 0, unroll=True)
    forward[1]()
    lax.fori_loop(first, chunks, local_output, 0, unroll=2)

    def transposed(c, carry):
        scores = dot(k[rows(c), :], q[rows(c), :], 1, 1)
        attn_t[c] = jnp.where(row <= column, scores, 0.0).astype(BF16)
        q_t[c] = q[rows(c), :].T
        return carry

    lax.fori_loop(0, chunks, transposed, 0, unroll=2)
    loads[3].wait()
    loads[4].wait()
    forward[2]()
    forward[3](earlier)

    eye_row, eye_column = iota2(HEAD_DIM, HEAD_DIM)
    eye = eye_row == eye_column
    gain = gain_ref[...]
    earlier16 = earlier[...].astype(BF16)

    def stat_copy(piece, slot, to):
        return pltpu.make_async_remote_copy(
            stats.at[piece], stat_slots.at[piece, slot],
            stat_s.at[piece, to], stat_r.at[piece, slot],
            device_id={"head": to}, device_id_type=MESH,
        )

    for piece in reversed(range(PIECES)):

        def finish_output(i, carry, piece=piece):
            c = piece * per_piece + i
            output = out32[rows(c), :] + dot(q[rows(c), :], earlier16, 1, 0)
            out32[rows(c), :] = output
            scaled = g[rows(c), :].astype(F32) * gain
            square = jnp.sum(output * output, axis=1, keepdims=True)
            product = jnp.sum(scaled * output, axis=1, keepdims=True)
            for n in range(groups):
                part = slice(n * HEAD_DIM, (n + 1) * HEAD_DIM)
                stats[piece, pl.ds(i * groups + n, 1), :] = jnp.sum(
                    jnp.where(eye, square[part], 0.0), axis=0, keepdims=True
                )
                stats[piece, pl.ds(stat_rows + i * groups + n, 1), :] = jnp.sum(
                    jnp.where(eye, product[part], 0.0), axis=0, keepdims=True
                )
            return carry

        lax.fori_loop(0, per_piece, finish_output, 0, unroll=UNROLL)
        for step in range(1, heads):
            to = lax.rem(head_index + step, heads)
            stat_copy(piece, head_index, to).start()

    running = jnp.zeros((HEAD_DIM, HEAD_DIM), F32)
    for piece in reversed(range(PIECES)):
        total = stats[piece]
        for step in range(1, heads):
            source = lax.rem(head_index + step, heads)
            stat_copy(piece, source, source).wait_recv()
            total = total + stat_slots[piece, source]
        total = total * (1.0 / width_all)
        rstd = lax.rsqrt(total[:stat_rows] + EPS)
        scale_rows[piece, :stat_rows] = rstd
        scale_rows[piece, stat_rows:] = rstd * rstd * rstd * total[stat_rows:]

        def gradient(i, running, piece=piece):
            def columns(offset):
                return jnp.concatenate(
                    [
                        jnp.sum(
                            jnp.where(eye, scale_rows[piece, pl.ds(offset + n, 1), :], 0.0),
                            axis=1, keepdims=True,
                        )
                        for n in range(groups)
                    ],
                    axis=0,
                )

            at = per_piece - 1 - i
            c = piece * per_piece + at
            rstd_c = columns(at * groups)
            output = out32[rows(c), :]
            scaled = g[rows(c), :].astype(F32) * gain
            grad = (rstd_c * scaled - output * columns(stat_rows + at * groups)).astype(BF16)
            dout[rows(c), :] = grad
            out32[rows(c), :] = output * rstd_c
            after[c] = running
            return running + dot(q_t[c], grad, 1, 0)

        running = lax.fori_loop(0, per_piece, gradient, running, unroll=UNROLL)

    total_b[...] = running
    backward[0]()

    def local_gradients(c, carry):
        grad = dout[rows(c), :]
        value = v[rows(c), :]
        prefix = (earlier[...] + before[c]).astype(BF16)
        suffix = after[c].astype(BF16)
        bmat = jnp.where(row >= column, dot(grad, value, 1, 1), 0.0).astype(BF16)
        bmat_t = jnp.where(row <= column, dot(value, grad, 1, 1), 0.0).astype(BF16)
        qg[rows(c), :] = (
            dot(bmat, k[rows(c), :], 1, 0) + dot(grad, prefix, 1, 1)
        ).astype(BF16)
        kpart[rows(c), :] = dot(bmat_t, q[rows(c), :], 1, 0) + dot(value, suffix, 1, 1)
        vpart[rows(c), :] = dot(attn_t[c], grad, 1, 0) + dot(k[rows(c), :], suffix, 1, 0)
        normed[rows(c), :] = (out32[rows(c), :] * gain).astype(BF16)
        return carry

    lax.fori_loop(0, first, local_gradients, 0, unroll=True)
    backward[1]()
    lax.fori_loop(first, chunks, local_gradients, 0, unroll=2)
    backward[2]()
    backward[3](later)
    later16[...] = later[...].astype(BF16)
    forward[4]()
    backward[4]()
    for piece in range(PIECES):
        for step in range(1, heads):
            to = lax.rem(head_index + step, heads)
            stat_copy(piece, head_index, to).wait_send()


def last_kernel(
    normed, qg, kpart, vpart, later16, k, v, normed_hbm, qg_hbm, kg_hbm, vg_hbm, kg, vg, sem
):
    chunks = k.shape[0] // CHUNK
    parts = 4 if chunks % 4 == 0 else 1
    per_part = chunks // parts
    stores = [
        pltpu.make_async_copy(normed, normed_hbm, sem.at[0]),
        pltpu.make_async_copy(qg, qg_hbm, sem.at[1]),
    ]
    for store in stores:
        store.start()

    suffix = later16[...]

    def finish_gradients(c, carry):
        part = pl.ds(pl.multiple_of(c * CHUNK, CHUNK), CHUNK)
        kg[part, :] = (kpart[part, :] + dot(v[part, :], suffix, 1, 1)).astype(BF16)
        vg[part, :] = (vpart[part, :] + dot(k[part, :], suffix, 1, 0)).astype(BF16)
        return carry

    for i in range(parts):
        lax.fori_loop(i * per_part, (i + 1) * per_part, finish_gradients, 0, unroll=2)
        part = pl.ds(i * per_part * CHUNK, per_part * CHUNK)
        for n, (src, dst) in enumerate(((kg, kg_hbm), (vg, vg_hbm))):
            store = pltpu.make_async_copy(src.at[part], dst.at[part], sem.at[2 + 2 * i + n])
            store.start()
            stores.append(store)
    for store in stores:
        store.wait()


def body(queries, key_rows, value_rows, norm_gain, out_grad):
    tokens, width = queries.shape
    assert width == HEAD_DIM and tokens % CHUNK == 0
    chips = lax.axis_size("seq") // 2
    heads = lax.axis_size("head")
    chunks = tokens // CHUNK
    stat_rows = 2 * tokens // HEAD_DIM // PIECES
    wide = (tokens, width)
    square = (HEAD_DIM, HEAD_DIM)
    half = (HEAD_DIM // 2, HEAD_DIM)
    link = [
        pltpu.VMEM(square, F32),
        pltpu.VMEM(square, F32),
        pltpu.VMEM(half, F32),
        pltpu.VMEM((chips,) + half, F32),
        pltpu.VMEM(half, F32),
        pltpu.VMEM(half, F32),
        pltpu.VMEM(square, F32),
    ]
    hbm = pl.BlockSpec(memory_space=pltpu.HBM)
    vmem = pl.BlockSpec(memory_space=pltpu.VMEM)
    dma = pltpu.SemaphoreType.DMA
    held = pl.pallas_call(
        functools.partial(kernel, chips, heads, width * heads),
        out_shape=[
            jax.ShapeDtypeStruct(wide, BF16),
            jax.ShapeDtypeStruct(wide, BF16),
            jax.ShapeDtypeStruct(wide, F32),
            jax.ShapeDtypeStruct(wide, F32),
            jax.ShapeDtypeStruct(square, BF16),
            jax.ShapeDtypeStruct(wide, BF16),
            jax.ShapeDtypeStruct(wide, BF16),
        ],
        in_specs=[hbm] * 5,
        out_specs=[vmem] * 7,
        scratch_shapes=[
            pltpu.VMEM(wide, BF16),
            pltpu.VMEM(wide, BF16),
            pltpu.VMEM((1, width), F32),
            pltpu.VMEM(wide, F32),
            pltpu.VMEM((chunks, CHUNK, CHUNK), BF16),
            pltpu.VMEM((chunks, HEAD_DIM, CHUNK), BF16),
            pltpu.VMEM(wide, BF16),
            pltpu.VMEM((chunks,) + square, F32),
            pltpu.VMEM((chunks,) + square, F32),
            pltpu.VMEM((PIECES, stat_rows, HEAD_DIM), F32),
            pltpu.VMEM((PIECES, heads, stat_rows, HEAD_DIM), F32),
            pltpu.VMEM((PIECES, stat_rows, HEAD_DIM), F32),
        ]
        + link
        + link
        + [
            dma((5,)), dma((PIECES, heads)), dma((PIECES, heads)),
            dma((2,)), dma((2,)), dma((2, chips)), dma((2, chips)), dma((2,)), dma((2,)),
        ],
        compiler_params=pltpu.CompilerParams(
            collective_id=0, has_side_effects=True, vmem_limit_bytes=32 * 1024 * 1024
        ),
    )(*[
        pltpu.with_memory_space_constraint(array, pltpu.HBM)
        for array in (queries, key_rows, value_rows, norm_gain.reshape(1, width), out_grad)
    ])
    return pl.pallas_call(
        last_kernel,
        out_shape=[jax.ShapeDtypeStruct(wide, BF16)] * 4,
        in_specs=[vmem] * 7,
        out_specs=[hbm] * 4,
        scratch_shapes=[pltpu.VMEM(wide, BF16), pltpu.VMEM(wide, BF16), dma((10,))],
        compiler_params=pltpu.CompilerParams(vmem_limit_bytes=32 * 1024 * 1024),
    )(*held)


def solution(mesh):
    spec = P("seq", "head")
    return jax.shard_map(
        body,
        mesh=mesh,
        in_specs=(spec, spec, spec, P("head"), spec),
        out_specs=(spec,) * 4,
        check_vma=False,
    )
```

```python
import functools

import jax
import jax.numpy as jnp
from jax import lax
from jax.experimental import pallas as pl
from jax.experimental.pallas import tpu as pltpu
from jax.sharding import PartitionSpec as P

HEAD_DIM = 128
CHUNK = 256
PIECES = 2
UNROLL = 4
SHARE = 32
EPS = 1e-05
MESH = pl.DeviceIdType.MESH
F32 = jnp.float32
BF16 = jnp.bfloat16


def dot(a, b, dim_a, dim_b):
    return lax.dot_general(a, b, (((dim_a,), (dim_b,)), ((), ())), preferred_element_type=F32)


def iota2(rows, columns):
    return (
        lax.broadcasted_iota(jnp.int32, (rows, columns), 0),
        lax.broadcasted_iota(jnp.int32, (rows, columns), 1),
    )


def exchange(total, pair_in, half_out, slots, half_acc, half_in, sems, chip, core, chips, upward):
    pair_s, pair_r, chip_s, chip_r, half_s, half_r = sems
    share = half_out.shape[0]
    rest = pl.ds(2 * share, HEAD_DIM - 2 * share)
    slot_share = pl.ds(0, share)
    slot_rest = pl.ds(share, HEAD_DIM - 2 * share)
    mine = pl.ds(pl.multiple_of(core * share, share), share)
    others = pl.ds(pl.multiple_of((1 - core) * share, share), share)
    partner = {"seq": chip * 2 + (1 - core)}

    def pair_copy():
        return pltpu.make_async_remote_copy(
            total, pair_in, pair_s, pair_r, device_id=partner, device_id_type=MESH
        )

    def share_copy(slot, to):
        return pltpu.make_async_remote_copy(
            half_out, slots.at[slot, slot_share], chip_s.at[to, 0], chip_r.at[slot, 0],
            device_id={"seq": to * 2 + core}, device_id_type=MESH,
        )

    def rest_copy(slot, to):
        return pltpu.make_async_remote_copy(
            total.at[rest], slots.at[slot, slot_rest], chip_s.at[to, 1], chip_r.at[slot, 1],
            device_id={"seq": to * 2 + core}, device_id_type=MESH,
        )

    def half_copy():
        return pltpu.make_async_remote_copy(
            half_acc, half_in, half_s, half_r, device_id=partner, device_id_type=MESH
        )

    def ahead(other):
        return (other > chip) if upward else (other < chip)

    def start_pair():
        pair_copy().start()
        for step in range(1, chips):
            to = lax.rem(chip + step, chips)

            @pl.when(ahead(to))
            def _():
                rest_copy(chip, to).start()

    def start_chips():
        pair_copy().wait_recv()
        half_out[...] = total[mine, :] + pair_in[mine, :]
        for step in range(1, chips):
            to = lax.rem(chip + step, chips)

            @pl.when(ahead(to))
            def _():
                share_copy(chip, to).start()

    def start_halves():
        half_acc[...] = jnp.zeros_like(half_acc)
        for source in range(chips):

            @pl.when(jnp.logical_and(jnp.logical_not(ahead(source)), source != chip))
            def _():
                rest_copy(source, source).wait_recv()
                share_copy(source, source).wait_recv()
                half_acc[...] += slots[source]

        half_copy().start()

    def finish(result):
        half_copy().wait_recv()
        result[mine, :] = half_acc[slot_share, :]
        result[others, :] = half_in[slot_share, :]
        result[rest, :] = half_acc[slot_rest, :] + half_in[slot_rest, :]

        @pl.when(core == (1 if upward else 0))
        def _():
            result[...] += pair_in[...]

    def drain():
        pair_copy().wait_send()
        for to in range(chips):

            @pl.when(ahead(to))
            def _():
                rest_copy(chip, to).wait_send()
                share_copy(chip, to).wait_send()

        half_copy().wait_send()

    return start_pair, start_chips, start_halves, finish, drain


def kernel(
    chips, heads, width_all,
    q_hbm, k_hbm, v_hbm, gain_hbm, g_hbm,
    normed, qg, kpart, vpart, later16, k, v,
    q, g, gain_ref,
    out32, attn_t, q_t, dout, before, after,
    stats, stat_slots, scale_rows,
    total_f, pair_f, hout_f, slots_f, hacc_f, hin_f, earlier,
    total_b, pair_b, hout_b, slots_b, hacc_b, hin_b, later,
    in_sem, stat_s, stat_r,
    pair_s, pair_r, chip_s, chip_r, half_s, half_r,
):
    seq_index = lax.axis_index("seq")
    head_index = lax.axis_index("head")
    chip = lax.div(seq_index, 2)
    core = lax.rem(seq_index, 2)
    tokens = q.shape[0]
    chunks = tokens // CHUNK
    groups = CHUNK // HEAD_DIM
    per_piece = chunks // PIECES
    stat_rows = per_piece * groups

    barrier = pltpu.get_barrier_semaphore()
    pl.semaphore_signal(
        barrier, inc=1, device_id={"seq": chip * 2 + (1 - core)}, device_id_type=MESH
    )
    for step in range(1, chips):
        pl.semaphore_signal(
            barrier, inc=1,
            device_id={"seq": lax.rem(chip + step, chips) * 2 + core}, device_id_type=MESH,
        )
    for step in range(1, heads):
        pl.semaphore_signal(
            barrier, inc=1, device_id={"head": lax.rem(head_index + step, heads)},
            device_id_type=MESH,
        )

    loads = [
        pltpu.make_async_copy(src, dst, in_sem.at[i])
        for i, (src, dst) in enumerate(
            ((k_hbm, k), (v_hbm, v), (q_hbm, q), (g_hbm, g), (gain_hbm, gain_ref))
        )
    ]
    for load in loads:
        load.start()

    def rows(c):
        return pl.ds(pl.multiple_of(c * CHUNK, CHUNK), CHUNK)

    def sems(i):
        return (
            pair_s.at[i], pair_r.at[i], chip_s.at[i], chip_r.at[i], half_s.at[i], half_r.at[i]
        )

    forward = exchange(
        total_f, pair_f, hout_f, slots_f, hacc_f, hin_f, sems(0), chip, core, chips, True
    )
    backward = exchange(
        total_b, pair_b, hout_b, slots_b, hacc_b, hin_b, sems(1), chip, core, chips, False
    )

    loads[0].wait()
    loads[1].wait()
    running = jnp.zeros((HEAD_DIM, HEAD_DIM), F32)
    for c in range(chunks):
        before[c] = running
        running = running + dot(k[rows(c), :], v[rows(c), :], 0, 0)
    total_f[...] = running

    pl.semaphore_wait(barrier, 1 + (chips - 1) + (heads - 1))
    forward[0]()

    row, column = iota2(CHUNK, CHUNK)

    def local_output(c, carry):
        scores = dot(q[rows(c), :], k[rows(c), :], 1, 1)
        attn = jnp.where(row >= column, scores, 0.0).astype(BF16)
        out32[rows(c), :] = dot(attn, v[rows(c), :], 1, 0) + dot(
            q[rows(c), :], before[c].astype(BF16), 1, 0
        )
        return carry

    first = chunks // 4
    loads[2].wait()
    lax.fori_loop(0, first, local_output, 0, unroll=True)
    forward[1]()
    lax.fori_loop(first, chunks, local_output, 0, unroll=2)

    def transposed(c, carry):
        scores = dot(k[rows(c), :], q[rows(c), :], 1, 1)
        attn_t[c] = jnp.where(row <= column, scores, 0.0).astype(BF16)
        q_t[c] = q[rows(c), :].T
        return carry

    lax.fori_loop(0, chunks, transposed, 0, unroll=2)
    loads[3].wait()
    loads[4].wait()
    forward[2]()
    forward[3](earlier)

    eye_row, eye_column = iota2(HEAD_DIM, HEAD_DIM)
    eye = eye_row == eye_column
    gain = gain_ref[...]
    earlier16 = earlier[...].astype(BF16)

    def stat_copy(piece, slot, to):
        return pltpu.make_async_remote_copy(
            stats.at[piece], stat_slots.at[piece, slot],
            stat_s.at[piece, to], stat_r.at[piece, slot],
            device_id={"head": to}, device_id_type=MESH,
        )

    for piece in reversed(range(PIECES)):

        def finish_output(i, carry, piece=piece):
            c = piece * per_piece + i
            output = out32[rows(c), :] + dot(q[rows(c), :], earlier16, 1, 0)
            out32[rows(c), :] = output
            scaled = g[rows(c), :].astype(F32) * gain
            square = jnp.sum(output * output, axis=1, keepdims=True)
            product = jnp.sum(scaled * output, axis=1, keepdims=True)
            for n in range(groups):
                part = slice(n * HEAD_DIM, (n + 1) * HEAD_DIM)
                stats[piece, pl.ds(i * groups + n, 1), :] = jnp.sum(
                    jnp.where(eye, square[part], 0.0), axis=0, keepdims=True
                )
                stats[piece, pl.ds(stat_rows + i * groups + n, 1), :] = jnp.sum(
                    jnp.where(eye, product[part], 0.0), axis=0, keepdims=True
                )
            return carry

        lax.fori_loop(0, per_piece, finish_output, 0, unroll=UNROLL)
        for step in range(1, heads):
            to = lax.rem(head_index + step, heads)
            stat_copy(piece, head_index, to).start()

    running = jnp.zeros((HEAD_DIM, HEAD_DIM), F32)
    for piece in reversed(range(PIECES)):
        total = stats[piece]
        for step in range(1, heads):
            source = lax.rem(head_index + step, heads)
            stat_copy(piece, source, source).wait_recv()
            total = total + stat_slots[piece, source]
        total = total * (1.0 / width_all)
        rstd = lax.rsqrt(total[:stat_rows] + EPS)
        scale_rows[piece, :stat_rows] = rstd
        scale_rows[piece, stat_rows:] = rstd * rstd * rstd * total[stat_rows:]

        def gradient(i, running, piece=piece):
            def columns(offset):
                return jnp.concatenate(
                    [
                        jnp.sum(
                            jnp.where(eye, scale_rows[piece, pl.ds(offset + n, 1), :], 0.0),
                            axis=1, keepdims=True,
                        )
                        for n in range(groups)
                    ],
                    axis=0,
                )

            at = per_piece - 1 - i
            c = piece * per_piece + at
            rstd_c = columns(at * groups)
            output = out32[rows(c), :]
            scaled = g[rows(c), :].astype(F32) * gain
            grad = (rstd_c * scaled - output * columns(stat_rows + at * groups)).astype(BF16)
            dout[rows(c), :] = grad
            out32[rows(c), :] = output * rstd_c
            after[c] = running
            return running + dot(q_t[c], grad, 1, 0)

        running = lax.fori_loop(0, per_piece, gradient, running, unroll=UNROLL)

    total_b[...] = running
    backward[0]()

    def local_gradients(c, carry):
        grad = dout[rows(c), :]
        value = v[rows(c), :]
        prefix = (earlier[...] + before[c]).astype(BF16)
        suffix = after[c].astype(BF16)
        bmat = jnp.where(row >= column, dot(grad, value, 1, 1), 0.0).astype(BF16)
        bmat_t = jnp.where(row <= column, dot(value, grad, 1, 1), 0.0).astype(BF16)
        qg[rows(c), :] = (
            dot(bmat, k[rows(c), :], 1, 0) + dot(grad, prefix, 1, 1)
        ).astype(BF16)
        kpart[rows(c), :] = dot(bmat_t, q[rows(c), :], 1, 0) + dot(value, suffix, 1, 1)
        vpart[rows(c), :] = dot(attn_t[c], grad, 1, 0) + dot(k[rows(c), :], suffix, 1, 0)
        normed[rows(c), :] = (out32[rows(c), :] * gain).astype(BF16)
        return carry

    lax.fori_loop(0, first, local_gradients, 0, unroll=True)
    backward[1]()
    lax.fori_loop(first, chunks, local_gradients, 0, unroll=2)
    backward[2]()
    backward[3](later)
    later16[...] = later[...].astype(BF16)
    forward[4]()
    backward[4]()
    for piece in range(PIECES):
        for step in range(1, heads):
            to = lax.rem(head_index + step, heads)
            stat_copy(piece, head_index, to).wait_send()


def last_kernel(
    normed, qg, kpart, vpart, later16, k, v, normed_hbm, qg_hbm, kg_hbm, vg_hbm, kg, vg, sem
):
    chunks = k.shape[0] // CHUNK
    parts = 4 if chunks % 4 == 0 else 1
    per_part = chunks // parts
    stores = [
        pltpu.make_async_copy(normed, normed_hbm, sem.at[0]),
        pltpu.make_async_copy(qg, qg_hbm, sem.at[1]),
    ]
    for store in stores:
        store.start()

    suffix = later16[...]

    def finish_gradients(c, carry):
        part = pl.ds(pl.multiple_of(c * CHUNK, CHUNK), CHUNK)
        kg[part, :] = (kpart[part, :] + dot(v[part, :], suffix, 1, 1)).astype(BF16)
        vg[part, :] = (vpart[part, :] + dot(k[part, :], suffix, 1, 0)).astype(BF16)
        return carry

    for i in range(parts):
        lax.fori_loop(i * per_part, (i + 1) * per_part, finish_gradients, 0, unroll=2)
        part = pl.ds(i * per_part * CHUNK, per_part * CHUNK)
        for n, (src, dst) in enumerate(((kg, kg_hbm), (vg, vg_hbm))):
            store = pltpu.make_async_copy(src.at[part], dst.at[part], sem.at[2 + 2 * i + n])
            store.start()
            stores.append(store)
    for store in stores:
        store.wait()


def body(queries, key_rows, value_rows, norm_gain, out_grad):
    tokens, width = queries.shape
    assert width == HEAD_DIM and tokens % CHUNK == 0
    chips = lax.axis_size("seq") // 2
    heads = lax.axis_size("head")
    chunks = tokens // CHUNK
    stat_rows = 2 * tokens // HEAD_DIM // PIECES
    wide = (tokens, width)
    square = (HEAD_DIM, HEAD_DIM)
    share = (SHARE, HEAD_DIM)
    swapped = (HEAD_DIM - SHARE, HEAD_DIM)
    link = [
        pltpu.VMEM(square, F32),
        pltpu.VMEM(square, F32),
        pltpu.VMEM(share, F32),
        pltpu.VMEM((chips,) + swapped, F32),
        pltpu.VMEM(swapped, F32),
        pltpu.VMEM(swapped, F32),
        pltpu.VMEM(square, F32),
    ]
    hbm = pl.BlockSpec(memory_space=pltpu.HBM)
    vmem = pl.BlockSpec(memory_space=pltpu.VMEM)
    dma = pltpu.SemaphoreType.DMA
    held = pl.pallas_call(
        functools.partial(kernel, chips, heads, width * heads),
        out_shape=[
            jax.ShapeDtypeStruct(wide, BF16),
            jax.ShapeDtypeStruct(wide, BF16),
            jax.ShapeDtypeStruct(wide, F32),
            jax.ShapeDtypeStruct(wide, F32),
            jax.ShapeDtypeStruct(square, BF16),
            jax.ShapeDtypeStruct(wide, BF16),
            jax.ShapeDtypeStruct(wide, BF16),
        ],
        in_specs=[hbm] * 5,
        out_specs=[vmem] * 7,
        scratch_shapes=[
            pltpu.VMEM(wide, BF16),
            pltpu.VMEM(wide, BF16),
            pltpu.VMEM((1, width), F32),
            pltpu.VMEM(wide, F32),
            pltpu.VMEM((chunks, CHUNK, CHUNK), BF16),
            pltpu.VMEM((chunks, HEAD_DIM, CHUNK), BF16),
            pltpu.VMEM(wide, BF16),
            pltpu.VMEM((chunks,) + square, F32),
            pltpu.VMEM((chunks,) + square, F32),
            pltpu.VMEM((PIECES, stat_rows, HEAD_DIM), F32),
            pltpu.VMEM((PIECES, heads, stat_rows, HEAD_DIM), F32),
            pltpu.VMEM((PIECES, stat_rows, HEAD_DIM), F32),
        ]
        + link
        + link
        + [
            dma((5,)), dma((PIECES, heads)), dma((PIECES, heads)),
            dma((2,)), dma((2,)), dma((2, chips, 2)), dma((2, chips, 2)), dma((2,)), dma((2,)),
        ],
        compiler_params=pltpu.CompilerParams(
            collective_id=0, has_side_effects=True, vmem_limit_bytes=32 * 1024 * 1024
        ),
    )(*[
        pltpu.with_memory_space_constraint(array, pltpu.HBM)
        for array in (queries, key_rows, value_rows, norm_gain.reshape(1, width), out_grad)
    ])
    return pl.pallas_call(
        last_kernel,
        out_shape=[jax.ShapeDtypeStruct(wide, BF16)] * 4,
        in_specs=[vmem] * 7,
        out_specs=[hbm] * 4,
        scratch_shapes=[pltpu.VMEM(wide, BF16), pltpu.VMEM(wide, BF16), dma((10,))],
        compiler_params=pltpu.CompilerParams(vmem_limit_bytes=32 * 1024 * 1024),
    )(*held)


def solution(mesh):
    spec = P("seq", "head")
    return jax.shard_map(
        body,
        mesh=mesh,
        in_specs=(spec, spec, spec, P("head"), spec),
        out_specs=(spec,) * 4,
        check_vma=False,
    )
```
